32 devices in a mesh: acq: 4 (over y, core), tile: 8 (over z, x).
Axes of the slice: x: 2, y: 2, z: 4, core: 2. Of those that a mesh axis runs over, the one named last changes fastest.
Arguments:
- slc: bfloat16 [32, 2, 64, 8192], P(('acq', 'tile'))
- offsets: int32 [32, 64], replicated, may hold values from -256 to 255
- partners: int32 [32, 4], replicated, may hold values from 0 to 31, as said below
Outputs:
- interferogram: float32 [2, 32, 4, 16, 512], P(None, 'acq', None, None, 'tile')
- coherence: float32 [32, 4, 16, 512], P('acq', None, None, 'tile')
The draws below stay inside these ranges and needn't reach their ends.
Inputs may be any that keep to these rules, and one draw needn't show every extreme that they name: partners[i, k] differs from i by 1 to 6; some pair of every draw lies exactly 6 acquisitions forward and some exactly 6 backward.
All inputs are finite; a program needn't handle non-finite values.
Results may differ from the reference program's by a relative error of at most 0.003.
Values may be sent and summed in bfloat16 or wider, within the bound.
A program may use at most 128 MiB of HBM per device.

```python
import jax
import jax.numpy as jnp
from jax import lax

AZ = 64
NP = 4
MAXGAP = 6
TAPS = 8
PHASES = 64
LA = 4
LR = 16
RG = 8192
NACQ = 32


def draw_slc(key, part):
    scene_key = jax.random.fold_in(key, 11)
    noise_key = jax.random.fold_in(key, 12)
    amp_key = jax.random.fold_in(key, 13)
    scene = jax.random.normal(scene_key, (1, 2, AZ, RG), jnp.float32)
    noise = jax.random.normal(noise_key, (NACQ, 2, AZ, RG), jnp.float32)
    amplitude = jnp.exp(jax.random.uniform(amp_key, (1, 1, AZ, RG), jnp.float32, jnp.log(0.3), jnp.log(3.0)))
    return (amplitude * (0.8 * scene + 0.6 * noise)).astype(jnp.bfloat16)


def draw_partners(key, part):
    rows_index = jnp.arange(NACQ, dtype=jnp.int32)[:, None]
    slot_index = jnp.arange(NP, dtype=jnp.int32)[None, :]
    magnitude = jax.random.randint(jax.random.fold_in(key, 21), (NACQ, NP), 1, MAXGAP + 1, jnp.int32)
    direction = jax.random.randint(jax.random.fold_in(key, 22), (NACQ, NP), 0, 2, jnp.int32) * 2 - 1
    target = rows_index + direction * magnitude
    outside = (target < 0) | (target > NACQ - 1)
    target = jnp.where(outside, rows_index - direction * magnitude, target)
    forward_slot = jax.random.randint(jax.random.fold_in(key, 23), (), 0, NP, jnp.int32)
    backward_slot = jax.random.randint(jax.random.fold_in(key, 24), (), 0, NP, jnp.int32)
    target = jnp.where((rows_index == NACQ - 1 - MAXGAP) & (slot_index == forward_slot), NACQ - 1, target)
    target = jnp.where((rows_index == MAXGAP) & (slot_index == backward_slot), 0, target)
    return target.astype(jnp.int32)


def with_ends(result, stream_key, least, top_value):
    longest = result.shape.index(max(result.shape))
    spots = []
    for shift in (0, 1):
        where = [jax.random.randint(jax.random.fold_in(stream_key, axis), (), 0, length) for axis, length in enumerate(result.shape)]
        where[longest] = (where[longest] + shift) % result.shape[longest]
        spots.append(tuple(where))
    return result.at[spots[0]].set(least).at[spots[1]].set(top_value)


def setup_inputs(seed: int = 0) -> dict:
    keys = jax.random.split(jax.random.key(seed), 4)
    return {
        "slc": draw_slc(jax.random.fold_in(keys[3], 71), 0),
        "offsets": with_ends(jax.random.randint(keys[1], (NACQ, AZ), -(TAPS // 2) * PHASES, (TAPS // 2) * PHASES), jax.random.fold_in(keys[1], 1), -(TAPS // 2) * PHASES, ((TAPS // 2) * PHASES) - 1).astype(jnp.int32),
        "partners": draw_partners(jax.random.fold_in(keys[3], 71), 0),
    }


def kernel_table():
    phase_grid = jnp.arange(PHASES, dtype=jnp.float32)[:, None]
    tap_grid = jnp.arange(TAPS, dtype=jnp.float32)[None, :]
    spot = tap_grid - (TAPS // 2 - 1) - phase_grid / PHASES
    window = 0.5 * (1.0 + jnp.cos(jnp.pi * spot / (TAPS // 2)))
    raw_kernel = jnp.sinc(spot) * window
    return raw_kernel / lax.optimization_barrier(jnp.sum(raw_kernel, axis=1, keepdims=True))

def shift_weights(offset_rows, kernel):
    whole_shift = offset_rows // PHASES
    phase_index = offset_rows - whole_shift * PHASES
    onehot = (phase_index[..., None] == jnp.arange(PHASES, dtype=jnp.int32)).astype(jnp.float32)
    flat = onehot.reshape(-1, PHASES)
    tap_weights = jnp.dot(flat, kernel, precision=lax.Precision.HIGHEST).reshape(offset_rows.shape + (TAPS,))
    positions = whole_shift[..., None] + jnp.arange(TAPS, dtype=jnp.int32) - (TAPS // 2 - 1)
    shifts = jnp.arange(2 * TAPS - 1, dtype=jnp.int32) - (TAPS - 1)
    matches = (positions[..., None] == shifts).astype(jnp.float32)
    return lax.optimization_barrier(jnp.sum(tap_weights[..., None] * matches, axis=-2))

def resample(padded, weights, out_width):
    running = jnp.zeros(padded.shape[:-1] + (out_width,), jnp.float32)
    for offset_index in range(2 * TAPS - 1):
        factor = weights[..., offset_index][..., None, :, None]
        running = running + factor * padded[..., offset_index:offset_index + out_width].astype(jnp.float32)
    return running.astype(jnp.bfloat16)

def multilook(values):
    item_count, az_rows, rg_cols = values.shape
    shaped = values.reshape(item_count, az_rows // LA, LA, rg_cols // LR, LR)
    return lax.optimization_barrier(jnp.sum(shaped, axis=(2, 4))) / (LA * LR)

def products(first_slc, second_slc):
    first_re = first_slc[:, 0].astype(jnp.float32)
    first_im = first_slc[:, 1].astype(jnp.float32)
    second_re = second_slc[:, 0].astype(jnp.float32)
    second_im = second_slc[:, 1].astype(jnp.float32)
    mean_re = multilook(first_re * second_re + first_im * second_im)
    mean_im = multilook(first_im * second_re - first_re * second_im)
    mean_first = multilook(first_re * first_re + first_im * first_im)
    mean_second = multilook(second_re * second_re + second_im * second_im)
    magnitude = jnp.sqrt(mean_re * mean_re + mean_im * mean_im)
    coherent = magnitude / jnp.sqrt((mean_first + 1e-06) * (mean_second + 1e-06))
    return (jnp.stack([mean_re, mean_im]), coherent)

def reference(slc, offsets, partners):
    kernel = kernel_table()
    reach = TAPS - 1

    def resample_one(operands):
        acquisition, offset_rows = operands
        padded = jnp.pad(acquisition, ((0, 0), (0, 0), (reach, reach)))
        return resample(padded, shift_weights(offset_rows, kernel), acquisition.shape[-1])
    resampled = lax.map(resample_one, (slc, offsets))

    def pair_one(operands):
        acquisition, chosen = operands
        partner_slc = jnp.take(resampled, chosen, axis=0)
        return products(jnp.broadcast_to(acquisition, partner_slc.shape), partner_slc)
    looked, coherent = lax.map(pair_one, (resampled, partners))
    return (jnp.transpose(looked, (1, 0, 2, 3, 4)), coherent)
```

```python
import functools

import jax
import jax.numpy as jnp
import numpy as np
from jax import lax
from jax.experimental import pallas as pl
from jax.experimental.pallas import tpu as pltpu
from jax.sharding import PartitionSpec as P

MAXGAP = 6
TAPS = 8
PHASES = 64
LA = 4
LR = 16
LANES = 128
CHUNKS = 4
STRIP = 512
DEVICE = pl.DeviceIdType.MESH


def offset_table():
    spot = np.arange(TAPS)[None, :] - (TAPS // 2 - 1) - np.arange(PHASES)[:, None] / PHASES
    raw = np.sinc(spot) * 0.5 * (1.0 + np.cos(np.pi * spot / (TAPS // 2)))
    kernel = raw / raw.sum(axis=1, keepdims=True)
    table = np.zeros((TAPS * PHASES, LANES), np.float32)
    for row in range(TAPS * PHASES):
        whole = row // PHASES - TAPS // 2
        first = whole + TAPS // 2
        table[row, first : first + TAPS] = kernel[row % PHASES]
    return table


def flipped(index, mask, size):
    out = 0
    bit = 1
    while bit < size:
        out = out + ((index // bit + mask // bit) % 2) * bit
        bit *= 2
    return out


def weighted_shifts(window, weights):
    width = window.shape[1]

    def ahead(value, count):
        return value if count == 0 else pltpu.roll(value, (-count) % width, 1)

    near = [ahead(window, s) for s in (-1, 0, 1)]
    total = None
    for q in (-2, -1, 0, 1, 2):
        part = None
        for s in (-1, 0, 1):
            weight = weights(3 * q + s + TAPS - 1)
            term = near[s + 1] * weight
            part = term if part is None else part + term
        part = ahead(part, 3 * q)
        total = part if total is None else total + part
    return total


def kernel(
    offsets_ref, table_ref, partners_ref, slc_ref, looked_ref, coherent_ref,
    padded, weights, outgoing, pool, pool_power, cross_sum, power_sum, *rest,
):
    extended = rest[:CHUNKS]
    in_sem, own_sem, send_sem, recv_sem, up_send, up_recv, down_send, down_recv = rest[CHUNKS:]
    group = lax.axis_size("tile")
    groups = lax.axis_size("acq")
    tile = lax.axis_index("tile")
    acq = lax.axis_index("acq")
    parts, az_rows, rg_cols = slc_ref.shape[1:]
    cols = rg_cols // group
    width = cols // CHUNKS
    looks = cols // LR
    slots = group + 2 * MAXGAP
    has_down, has_up = acq > 0, acq < groups - 1

    load = pltpu.make_async_copy(slc_ref.at[0], padded.at[:, :, pl.ds(LANES, rg_cols)], in_sem)
    load.start()

    barrier = pltpu.get_barrier_semaphore()

    def greet(step, carry):
        other = flipped(tile, group - 1 - step, group)
        pl.semaphore_signal(barrier, inc=1, device_id=(acq, other), device_id_type=DEVICE)
        return carry

    lax.fori_loop(0, group - 1, greet, 0)

    @pl.when(has_down)
    def _():
        pl.semaphore_signal(barrier, inc=1, device_id=(acq - 1, tile), device_id_type=DEVICE)

    @pl.when(has_up)
    def _():
        pl.semaphore_signal(barrier, inc=1, device_id=(acq + 1, tile), device_id_type=DEVICE)

    own = offsets_ref[pl.ds(acq * group + tile, 1), :]
    rows = lax.broadcasted_iota(jnp.int32, (TAPS * PHASES, az_rows), 0)
    onehot = jnp.where(rows == own + TAPS // 2 * PHASES, 1.0, 0.0).astype(jnp.float32)
    found = lax.dot_general(
        onehot, table_ref[...], (((0,), (0,)), ((), ())),
        precision=lax.Precision.HIGHEST, preferred_element_type=jnp.float32,
    )
    for d in range(2 * TAPS - 1):
        weights[d] = jnp.broadcast_to(found[:, d : d + 1], (az_rows, LANES))
    edge = jnp.zeros((parts, az_rows, LANES), padded.dtype)
    padded[:, :, pl.ds(0, LANES)] = edge
    padded[:, :, pl.ds(LANES + rg_cols, LANES)] = edge

    load.wait()

    greeted = jnp.where(has_down, 1, 0) + jnp.where(has_up, 1, 0)
    pl.semaphore_wait(barrier, group - 1 + greeted)

    def to_tile(step, chunk, other):
        return pltpu.make_async_remote_copy(
            src_ref=outgoing.at[step, chunk],
            dst_ref=extended[chunk].at[MAXGAP + tile],
            send_sem=send_sem.at[chunk, step],
            recv_sem=recv_sem.at[chunk, tile],
            device_id=(acq, other),
            device_id_type=DEVICE,
        )

    def from_tile(step, chunk, other):
        return pltpu.make_async_remote_copy(
            src_ref=outgoing.at[step, chunk],
            dst_ref=extended[chunk].at[MAXGAP + other],
            send_sem=send_sem.at[chunk, step],
            recv_sem=recv_sem.at[chunk, other],
            device_id=(acq, other),
            device_id_type=DEVICE,
        )

    def keep(chunk):
        return pltpu.make_async_copy(
            outgoing.at[group - 1, chunk], extended[chunk].at[MAXGAP + tile], own_sem.at[chunk]
        )

    def resample(step, carry):
        other = flipped(tile, group - 1 - step, group)
        begin = pl.multiple_of(other * cols, LANES)

        def row_block(index, inner):
            part = index // (az_rows // 16)
            row = pl.multiple_of(index % (az_rows // 16) * 16, 16)
            for strip in range(cols // STRIP):
                start = pl.multiple_of(begin + strip * STRIP, LANES)
                span = STRIP + 2 * LANES
                window = padded[part, pl.ds(row, 16), pl.ds(start, span)].astype(jnp.float32)

                def weight(d):
                    return jnp.concatenate([weights[d, pl.ds(row, 16), :]] * (span // LANES), axis=1)

                total = weighted_shifts(window, weight)[:, LANES : LANES + STRIP].astype(jnp.bfloat16)
                for piece in range(STRIP // width):
                    outgoing[step, strip * (STRIP // width) + piece, part, pl.ds(row, 16), :] = total[
                        :, piece * width : (piece + 1) * width
                    ]
            return inner

        lax.fori_loop(0, parts * (az_rows // 16), row_block, 0)

        @pl.when(step < group - 1)
        def _():
            to_tile(step, 0, other).start()

        return carry

    lax.fori_loop(0, group, resample, 0)
    for chunk in range(CHUNKS):
        keep(chunk).start()
        if chunk:

            def send(step, carry, chunk=chunk):
                to_tile(step, chunk, flipped(tile, group - 1 - step, group)).start()
                return carry

            lax.fori_loop(0, group - 1, send, 0)

    for chunk in range(CHUNKS):
        for quarter in range(4):
            spot = (lax.broadcasted_iota(jnp.int32, (width, 2 * looks), 0) + chunk * width) // LR
            lane = lax.broadcasted_iota(jnp.int32, (width, 2 * looks), 1)
            hit = jnp.where(lane == spot + (looks if quarter >= 2 else 0), 1.0, 0.0)
            pool[chunk, quarter * width : (quarter + 1) * width] = (
                -hit if quarter == 3 else hit
            ).astype(jnp.bfloat16)
            if quarter < 2:
                both = jnp.where((lane == spot) | (lane == spot + looks), 1.0, 0.0)
                pool_power[chunk, quarter * width : (quarter + 1) * width] = both.astype(jnp.bfloat16)

    def up(chunk, source):
        return pltpu.make_async_remote_copy(
            src_ref=extended[chunk].at[MAXGAP + source],
            dst_ref=extended[chunk].at[source - (group - MAXGAP)],
            send_sem=up_send.at[chunk, source - (group - MAXGAP)],
            recv_sem=up_recv.at[chunk, source - (group - MAXGAP)],
            device_id=(acq + 1, tile),
            device_id_type=DEVICE,
        )

    def down(chunk, source):
        return pltpu.make_async_remote_copy(
            src_ref=extended[chunk].at[MAXGAP + source],
            dst_ref=extended[chunk].at[MAXGAP + group + source],
            send_sem=down_send.at[chunk, source],
            recv_sem=down_recv.at[chunk, source],
            device_id=(acq - 1, tile),
            device_id_type=DEVICE,
        )

    def hand_on(chunk, source):
        @pl.when(has_up & (source >= group - MAXGAP))
        def _():
            up(chunk, source).start()

        @pl.when(has_down & (source < MAXGAP))
        def _():
            down(chunk, source).start()

    def relay(chunk):
        keep(chunk).wait()
        hand_on(chunk, tile)

        def one(index, carry):
            step = group - 2 - index
            source = flipped(tile, group - 1 - step, group)
            from_tile(step, chunk, source).wait_recv()
            hand_on(chunk, source)
            return carry

        lax.fori_loop(0, group - 1, one, 0)

    def gathered(chunk):
        @pl.when(has_down)
        def _():
            def one(index, carry):
                up(chunk, index + group - MAXGAP).wait_recv()
                return carry

            lax.fori_loop(0, MAXGAP, one, 0)

        @pl.when(has_up)
        def _():
            def one(index, carry):
                down(chunk, index).wait_recv()
                return carry

            lax.fori_loop(0, MAXGAP, one, 0)

    def slot_of(owner, k):
        return jnp.clip(partners_ref[acq * group + owner, k] - acq * group + MAXGAP, 0, slots - 1)

    def pairs(chunk):
        images = extended[chunk]

        def powers(index, carry):
            squares = []
            for k in range(4):
                image = images[index * 4 + k]
                squares.append(jnp.concatenate([image[0] * image[0], image[1] * image[1]], axis=1))
            pooled = jnp.dot(
                jnp.concatenate(squares, axis=0), pool_power[chunk], preferred_element_type=jnp.float32
            ).reshape(4, az_rows, 2 * looks)
            span = pl.ds(index * 4, 4)
            power_sum[span] = pooled if chunk == 0 else power_sum[span] + pooled
            return carry

        lax.fori_loop(0, slots // 4, powers, 0)

        def crosses(owner, carry):
            first = images[MAXGAP + owner]
            blocks = []
            for k in range(partners_ref.shape[1]):
                second = images[slot_of(owner, k)]
                blocks.append(
                    jnp.concatenate(
                        [first[0] * second[0], first[1] * second[1], first[1] * second[0], first[0] * second[1]],
                        axis=1,
                    )
                )
            pooled = jnp.dot(
                jnp.concatenate(blocks, axis=0), pool[chunk], preferred_element_type=jnp.float32
            ).reshape(len(blocks), az_rows, 2 * looks)
            cross_sum[owner] = pooled if chunk == 0 else cross_sum[owner] + pooled
            return carry

        lax.fori_loop(0, group, crosses, 0)

    relay(0)
    for chunk in range(CHUNKS):
        gathered(chunk)
        pairs(chunk)
        if chunk + 1 < CHUNKS:
            relay(chunk + 1)

    windows = az_rows // LA

    def mean(view, *lead):
        total = None
        for line in range(LA):
            value = view[(*lead, pl.ds(line, windows, stride=LA), slice(None))]
            total = value if total is None else total + value
        return total * (1.0 / (LA * LR))

    def finish(owner, carry):
        mean_a = mean(power_sum, MAXGAP + owner)
        for k in range(partners_ref.shape[1]):
            mean_b = mean(power_sum, slot_of(owner, k))
            cross = mean(cross_sum, owner, k)
            square = cross * cross
            magnitude = jnp.sqrt(square + pltpu.roll(square, looks, 1))
            coherent = magnitude / jnp.sqrt((mean_a + 1e-06) * (mean_b + 1e-06))
            looked_ref[0, owner, k] = cross[:, :looks]
            looked_ref[1, owner, k] = pltpu.roll(cross, looks, 1)[:, :looks]
            coherent_ref[owner, k] = coherent[:, :looks]
        return carry

    lax.fori_loop(0, group, finish, 0)

    for chunk in range(CHUNKS):

        def sent(step, carry, chunk=chunk):
            to_tile(step, chunk, flipped(tile, group - 1 - step, group)).wait_send()
            return carry

        lax.fori_loop(0, group - 1, sent, 0)

        @pl.when(has_up)
        def _(chunk=chunk):
            def one(index, carry):
                up(chunk, index + group - MAXGAP).wait_send()
                return carry

            lax.fori_loop(0, MAXGAP, one, 0)

        @pl.when(has_down)
        def _(chunk=chunk):
            def one(index, carry):
                down(chunk, index).wait_send()
                return carry

            lax.fori_loop(0, MAXGAP, one, 0)


def body(group, slc, offsets, partners):
    _, parts, az_rows, rg_cols = slc.shape
    pair_count = partners.shape[1]
    cols = rg_cols // group
    width, looks = cols // CHUNKS, cols // LR
    slots = group + 2 * MAXGAP
    vmem = pl.BlockSpec(memory_space=pltpu.VMEM)
    dma = pltpu.SemaphoreType.DMA
    return pl.pallas_call(
        kernel,
        out_shape=(
            jax.ShapeDtypeStruct((2, group, pair_count, az_rows // LA, looks), jnp.float32),
            jax.ShapeDtypeStruct((group, pair_count, az_rows // LA, looks), jnp.float32),
        ),
        in_specs=[vmem, vmem, pl.BlockSpec(memory_space=pltpu.SMEM), pl.BlockSpec(memory_space=pl.ANY)],
        out_specs=(vmem, vmem),
        scratch_shapes=[
            pltpu.VMEM((parts, az_rows, rg_cols + 2 * LANES), jnp.bfloat16),
            pltpu.VMEM((2 * TAPS - 1, az_rows, LANES), jnp.float32),
            pltpu.VMEM((group, CHUNKS, parts, az_rows, width), jnp.bfloat16),
            pltpu.VMEM((CHUNKS, 4 * width, 2 * looks), jnp.bfloat16),
            pltpu.VMEM((CHUNKS, 2 * width, 2 * looks), jnp.bfloat16),
            pltpu.VMEM((group, pair_count, az_rows, 2 * looks), jnp.float32),
            pltpu.VMEM((slots, az_rows, 2 * looks), jnp.float32),
        ]
        + [pltpu.VMEM((slots, parts, az_rows, width), jnp.bfloat16)] * CHUNKS
        + [
            dma(()),
            dma((CHUNKS,)),
            dma((CHUNKS, group)),
            dma((CHUNKS, group)),
            dma((CHUNKS, MAXGAP)),
            dma((CHUNKS, MAXGAP)),
            dma((CHUNKS, MAXGAP)),
            dma((CHUNKS, MAXGAP)),
        ],
        compiler_params=pltpu.CompilerParams(
            collective_id=0, has_side_effects=True, vmem_limit_bytes=48 * 1024 * 1024
        ),
    )(offsets, jnp.asarray(offset_table()), partners, slc)


def solution(mesh):
    return jax.shard_map(
        functools.partial(body, mesh.shape["tile"]),
        mesh=mesh,
        in_specs=(P(("acq", "tile"), None, None, None), P(), P()),
        out_specs=(P(None, "acq", None, None, "tile"), P("acq", None, None, "tile")),
        check_vma=False,
    )
```

```python
import functools

import jax
import jax.numpy as jnp
from jax import lax
from jax.experimental import pallas as pl
from jax.experimental.pallas import tpu as pltpu
from jax.sharding import PartitionSpec as P

MAXGAP = 6
TAPS = 8
PHASES = 64
LA = 4
LR = 16
LANES = 128
SHARES = (1, 1, 1, 1)
CHUNKS = len(SHARES)
EARLY = 1
OWNERS = 4
DEVICE = pl.DeviceIdType.MESH


def chunk_spans(cols):
    unit = cols // sum(SHARES)
    return [(sum(SHARES[:c]) * unit, SHARES[c] * unit) for c in range(CHUNKS)]


def flipped(index, mask, size):
    out = 0
    bit = 1
    while bit < size:
        out = out + ((index // bit + mask // bit) % 2) * bit
        bit *= 2
    return out


def weighted_shifts(window, weights):
    width = window.shape[1]

    def ahead(value, count):
        return value if count == 0 else pltpu.roll(value, (-count) % width, 1)

    near = [ahead(window, s) for s in (-1, 0, 1)]
    total = None
    for q in (-2, -1, 0, 1, 2):
        part = None
        for s in (-1, 0, 1):
            weight = weights(3 * q + s + TAPS - 1)
            term = near[s + 1] * weight
            part = term if part is None else part + term
        part = ahead(part, 3 * q)
        total = part if total is None else total + part
    return total


def kernel(
    offsets_ref, partners_ref, slc_ref, looked_ref, coherent_ref,
    offsets, padded, weights, cross_sum, power_sum, *rest,
):
    extended, outgoing, pool, pool_power = (rest[i * CHUNKS : (i + 1) * CHUNKS] for i in range(4))
    fetch_sem, in_sem, own_sem, send_sem, recv_sem, up_send, up_recv, down_send, down_recv = rest[4 * CHUNKS :]
    group = lax.axis_size("tile")
    groups = lax.axis_size("acq")
    tile = lax.axis_index("tile")
    acq = lax.axis_index("acq")
    parts, az_rows, rg_cols = slc_ref.shape[1:]
    cols = rg_cols // group
    spans = chunk_spans(cols)
    looks = cols // LR
    slots = group + 2 * MAXGAP
    pair_count = partners_ref.shape[0]
    has_down, has_up = acq > 0, acq < groups - 1

    fetch = pltpu.make_async_copy(offsets_ref, offsets, fetch_sem)
    fetch.start()
    load = pltpu.make_async_copy(slc_ref.at[0], padded.at[:, :, pl.ds(LANES, rg_cols)], in_sem)
    load.start()

    barrier = pltpu.get_barrier_semaphore()

    def greet(step, carry):
        other = flipped(tile, group - 1 - step, group)
        pl.semaphore_signal(barrier, inc=1, device_id=(acq, other), device_id_type=DEVICE)
        return carry

    lax.fori_loop(0, group - 1, greet, 0)

    @pl.when(has_down)
    def _():
        pl.semaphore_signal(barrier, inc=1, device_id=(acq - 1, tile), device_id_type=DEVICE)

    @pl.when(has_up)
    def _():
        pl.semaphore_signal(barrier, inc=1, device_id=(acq + 1, tile), device_id_type=DEVICE)

    fetch.wait()
    own = jnp.broadcast_to(
        offsets[pl.ds(acq * group + tile, 1), :].astype(jnp.float32), (az_rows, az_rows)
    )
    diagonal = lax.broadcasted_iota(jnp.int32, (az_rows, az_rows), 0) == lax.broadcasted_iota(
        jnp.int32, (az_rows, az_rows), 1
    )
    own = jnp.sum(jnp.where(diagonal, own, 0.0), axis=1, keepdims=True)
    shift = lax.broadcasted_iota(jnp.int32, (az_rows, LANES), 1) - (TAPS - 1)
    spot = shift.astype(jnp.float32) - own * (1.0 / PHASES)
    angle = jnp.pi * spot
    sinc = jnp.where(spot == 0.0, 1.0, jnp.sin(angle) / jnp.where(spot == 0.0, 1.0, angle))
    raw = sinc * (0.5 * (1.0 + jnp.cos(angle * (2.0 / TAPS))))
    raw = jnp.where(jnp.abs(spot) < TAPS // 2, raw, 0.0)
    found = raw / jnp.sum(raw, axis=1, keepdims=True)
    for d in range(2 * TAPS - 1):
        weights[d] = jnp.broadcast_to(found[:, d : d + 1], (az_rows, LANES))
    edge = jnp.zeros((parts, az_rows, LANES), padded.dtype)
    padded[:, :, pl.ds(0, LANES)] = edge
    padded[:, :, pl.ds(LANES + rg_cols, LANES)] = edge

    load.wait()

    greeted = jnp.where(has_down, 1, 0) + jnp.where(has_up, 1, 0)
    pl.semaphore_wait(barrier, group - 1 + greeted)

    def to_tile(step, chunk, other):
        return pltpu.make_async_remote_copy(
            src_ref=outgoing[chunk].at[step],
            dst_ref=extended[chunk].at[MAXGAP + tile],
            send_sem=send_sem.at[chunk, step],
            recv_sem=recv_sem.at[chunk, tile],
            device_id=(acq, other),
            device_id_type=DEVICE,
        )

    def from_tile(step, chunk, other):
        return pltpu.make_async_remote_copy(
            src_ref=outgoing[chunk].at[step],
            dst_ref=extended[chunk].at[MAXGAP + other],
            send_sem=send_sem.at[chunk, step],
            recv_sem=recv_sem.at[chunk, other],
            device_id=(acq, other),
            device_id_type=DEVICE,
        )

    def keep(chunk):
        return pltpu.make_async_copy(
            outgoing[chunk].at[group - 1], extended[chunk].at[MAXGAP + tile], own_sem.at[chunk]
        )

    def resample(step, carry):
        other = flipped(tile, group - 1 - step, group)
        begin = pl.multiple_of(other * cols, LANES)

        def row_block(index, inner):
            part = index // (az_rows // 16)
            row = pl.multiple_of(index % (az_rows // 16) * 16, 16)
            span = cols + 2 * LANES
            window = padded[part, pl.ds(row, 16), pl.ds(begin, span)].astype(jnp.float32)

            def weight(half, d):
                return jnp.concatenate([weights[d, pl.ds(row + half, 8), :]] * (span // LANES), axis=1)

            total = jnp.concatenate(
                [
                    weighted_shifts(window[:8], functools.partial(weight, 0)),
                    weighted_shifts(window[8:], functools.partial(weight, 8)),
                ],
                axis=0,
            )[:, LANES : LANES + cols].astype(jnp.bfloat16)
            for chunk, (first, width) in enumerate(spans):
                outgoing[chunk][step, part, pl.ds(row, 16), :] = total[:, first : first + width]
            return inner

        lax.fori_loop(0, parts * (az_rows // 16), row_block, 0)

        @pl.when(step < group - 1)
        def _():
            to_tile(step, 0, other).start()

        return carry

    def send(chunk, begin, end):
        def one(step, carry):
            to_tile(group - 2 - step, chunk, flipped(tile, 1 + step, group)).start()
            return carry

        lax.fori_loop(begin, end, one, 0)

    lax.fori_loop(0, group // 2, resample, 0)
    for chunk in range(1, EARLY):
        send(chunk, 0, group // 2)
    lax.fori_loop(group // 2, group, resample, 0)
    for chunk in range(1, CHUNKS):
        send(chunk, group // 2 if chunk < EARLY else 0, group - 1)
    for chunk in range(CHUNKS):
        keep(chunk).start()

    for chunk, (first, width) in enumerate(spans):
        spot = (lax.broadcasted_iota(jnp.int32, (width, 2 * looks), 0) + first) // LR
        lane = lax.broadcasted_iota(jnp.int32, (width, 2 * looks), 1)
        left = jnp.where(lane == spot, 1.0, 0.0)
        right = jnp.where(lane == spot + looks, 1.0, 0.0)
        for quarter, block in enumerate((left, left, right, -right)):
            pool[chunk][quarter * width : (quarter + 1) * width] = block.astype(jnp.bfloat16)
        for half in range(2):
            pool_power[chunk][half * width : (half + 1) * width] = (left + right).astype(jnp.bfloat16)

    def up(chunk, source):
        return pltpu.make_async_remote_copy(
            src_ref=extended[chunk].at[MAXGAP + source],
            dst_ref=extended[chunk].at[source - (group - MAXGAP)],
            send_sem=up_send.at[chunk, source - (group - MAXGAP)],
            recv_sem=up_recv.at[chunk, source - (group - MAXGAP)],
            device_id=(acq + 1, tile),
            device_id_type=DEVICE,
        )

    def down(chunk, source):
        return pltpu.make_async_remote_copy(
            src_ref=extended[chunk].at[MAXGAP + source],
            dst_ref=extended[chunk].at[MAXGAP + group + source],
            send_sem=down_send.at[chunk, source],
            recv_sem=down_recv.at[chunk, source],
            device_id=(acq - 1, tile),
            device_id_type=DEVICE,
        )

    def hand_on(chunk, source):
        @pl.when(has_up & (source >= group - MAXGAP))
        def _():
            up(chunk, source).start()

        @pl.when(has_down & (source < MAXGAP))
        def _():
            down(chunk, source).start()

    def relay(chunk):
        keep(chunk).wait()
        hand_on(chunk, tile)

        def one(index, carry):
            step = group - 2 - index
            source = flipped(tile, group - 1 - step, group)
            from_tile(step, chunk, source).wait_recv()
            hand_on(chunk, source)
            return carry

        lax.fori_loop(0, group - 1, one, 0)

    def gathered(chunk):
        @pl.when(has_down)
        def _():
            def one(index, carry):
                up(chunk, index + group - MAXGAP).wait_recv()
                return carry

            lax.fori_loop(0, MAXGAP, one, 0)

        @pl.when(has_up)
        def _():
            def one(index, carry):
                down(chunk, index).wait_recv()
                return carry

            lax.fori_loop(0, MAXGAP, one, 0)

    def slot_of(owner, k):
        return jnp.clip(partners_ref[k, acq * group + owner] - acq * group + MAXGAP, 0, slots - 1)

    def pairs(chunk):
        images = extended[chunk]

        def powers(index, carry):
            squares = []
            for k in range(4):
                image = images[index * 4 + k]
                squares.append(jnp.concatenate([image[0] * image[0], image[1] * image[1]], axis=1))
            pooled = jnp.dot(
                jnp.concatenate(squares, axis=0), pool_power[chunk][...], preferred_element_type=jnp.float32
            ).reshape(4, az_rows, 2 * looks)
            span = pl.ds(index * 4, 4)
            power_sum[span] = pooled if chunk == 0 else power_sum[span] + pooled
            return carry

        lax.fori_loop(0, slots // 4, powers, 0)

        def crosses(index, carry):
            blocks = []
            for owner in (index * OWNERS + j for j in range(OWNERS)):
                first = images[MAXGAP + owner]
                for k in range(pair_count):
                    second = images[slot_of(owner, k)]
                    blocks.append(
                        jnp.concatenate(
                            [first[0] * second[0], first[1] * second[1], first[1] * second[0], first[0] * second[1]],
                            axis=1,
                        )
                    )
            pooled = jnp.dot(
                jnp.concatenate(blocks, axis=0), pool[chunk][...], preferred_element_type=jnp.float32
            ).reshape(OWNERS, pair_count, az_rows, 2 * looks)
            span = pl.ds(index * OWNERS, OWNERS)
            cross_sum[span] = pooled if chunk == 0 else cross_sum[span] + pooled
            return carry

        lax.fori_loop(0, group // OWNERS, crosses, 0)

    relay(0)
    for chunk in range(CHUNKS):
        if chunk + 1 < CHUNKS:
            relay(chunk + 1)
        gathered(chunk)
        pairs(chunk)

    windows = az_rows // LA

    def mean(view, *lead):
        total = None
        for line in range(LA):
            value = view[(*lead, pl.ds(line, windows, stride=LA), slice(None))]
            total = value if total is None else total + value
        return total * (1.0 / (LA * LR))

    def finish(owner):
        mean_a = mean(power_sum, MAXGAP + owner)
        for k in range(partners_ref.shape[0]):
            mean_b = mean(power_sum, slot_of(owner, k))
            cross = mean(cross_sum, owner, k)
            square = cross * cross
            magnitude = jnp.sqrt(square + pltpu.roll(square, looks, 1))
            coherent = magnitude / jnp.sqrt((mean_a + 1e-06) * (mean_b + 1e-06))
            looked_ref[0, owner, k] = cross[:, :looks]
            looked_ref[1, owner, k] = pltpu.roll(cross, looks, 1)[:, :looks]
            coherent_ref[owner, k] = coherent[:, :looks]

    @pl.loop(0, group // 2)
    def _(index):
        finish(index * 2)
        finish(index * 2 + 1)

    for chunk in range(CHUNKS):

        def sent(step, carry, chunk=chunk):
            to_tile(step, chunk, flipped(tile, group - 1 - step, group)).wait_send()
            return carry

        lax.fori_loop(0, group - 1, sent, 0)

        @pl.when(has_up)
        def _(chunk=chunk):
            def one(index, carry):
                up(chunk, index + group - MAXGAP).wait_send()
                return carry

            lax.fori_loop(0, MAXGAP, one, 0)

        @pl.when(has_down)
        def _(chunk=chunk):
            def one(index, carry):
                down(chunk, index).wait_send()
                return carry

            lax.fori_loop(0, MAXGAP, one, 0)


def body(group, slc, offsets, partners):
    _, parts, az_rows, rg_cols = slc.shape
    pair_count = partners.shape[1]
    cols = rg_cols // group
    looks = cols // LR
    widths = [width for _, width in chunk_spans(cols)]
    slots = group + 2 * MAXGAP
    vmem = pl.BlockSpec(memory_space=pltpu.VMEM)
    hbm = pl.BlockSpec(memory_space=pltpu.HBM)
    dma = pltpu.SemaphoreType.DMA
    return pl.pallas_call(
        kernel,
        out_shape=(
            jax.ShapeDtypeStruct((2, group, pair_count, az_rows // LA, looks), jnp.float32),
            jax.ShapeDtypeStruct((group, pair_count, az_rows // LA, looks), jnp.float32),
        ),
        in_specs=[hbm, pl.BlockSpec(memory_space=pltpu.SMEM), hbm],
        out_specs=(vmem, vmem),
        scratch_shapes=[
            pltpu.VMEM(offsets.shape, jnp.int32),
            pltpu.VMEM((parts, az_rows, rg_cols + 2 * LANES), jnp.bfloat16),
            pltpu.VMEM((2 * TAPS - 1, az_rows, LANES), jnp.float32),
            pltpu.VMEM((group, pair_count, az_rows, 2 * looks), jnp.float32),
            pltpu.VMEM((slots, az_rows, 2 * looks), jnp.float32),
        ]
        + [pltpu.VMEM((slots, parts, az_rows, width), jnp.bfloat16) for width in widths]
        + [pltpu.VMEM((group, parts, az_rows, width), jnp.bfloat16) for width in widths]
        + [pltpu.VMEM((4 * width, 2 * looks), jnp.bfloat16) for width in widths]
        + [pltpu.VMEM((2 * width, 2 * looks), jnp.bfloat16) for width in widths]
        + [
            dma(()),
            dma(()),
            dma((CHUNKS,)),
            dma((CHUNKS, group)),
            dma((CHUNKS, group)),
            dma((CHUNKS, MAXGAP)),
            dma((CHUNKS, MAXGAP)),
            dma((CHUNKS, MAXGAP)),
            dma((CHUNKS, MAXGAP)),
        ],
        compiler_params=pltpu.CompilerParams(
            collective_id=0, has_side_effects=True, vmem_limit_bytes=60 * 1024 * 1024
        ),
    )(offsets, partners.T, slc)


def solution(mesh):
    return jax.shard_map(
        functools.partial(body, mesh.shape["tile"]),
        mesh=mesh,
        in_specs=(P(("acq", "tile"), None, None, None), P(), P()),
        out_specs=(P(None, "acq", None, None, "tile"), P("acq", None, None, "tile")),
        check_vma=False,
    )
```

```python
import functools

import jax
import jax.numpy as jnp
from jax import lax
from jax.experimental import pallas as pl
from jax.experimental.pallas import tpu as pltpu
from jax.sharding import PartitionSpec as P

MAXGAP = 6
TAPS = 8
PHASES = 64
LA = 4
LR = 16
LANES = 128
SHARES = (1, 1, 1, 1)
CHUNKS = len(SHARES)
EARLY = 1
OWNERS = 8
DEVICE = pl.DeviceIdType.MESH


def chunk_spans(cols):
    unit = cols // sum(SHARES)
    return [(sum(SHARES[:c]) * unit, SHARES[c] * unit) for c in range(CHUNKS)]


def flipped(index, mask, size):
    out = 0
    bit = 1
    while bit < size:
        out = out + ((index // bit + mask // bit) % 2) * bit
        bit *= 2
    return out


def weighted_shifts(window, weights):
    width = window.shape[1]

    def ahead(value, count):
        return value if count == 0 else pltpu.roll(value, (-count) % width, 1)

    near = [ahead(window, s) for s in (-1, 0, 1)]
    total = None
    for q in (-2, -1, 0, 1, 2):
        part = None
        for s in (-1, 0, 1):
            weight = weights(3 * q + s + TAPS - 1)
            term = near[s + 1] * weight
            part = term if part is None else part + term
        part = ahead(part, 3 * q)
        total = part if total is None else total + part
    return total


def kernel(
    offsets_ref, partners_ref, slc_ref, looked_ref, coherent_ref,
    offsets, padded, weights, cross_sum, power_sum, *rest,
):
    extended, outgoing, pool, pool_power = (rest[i * CHUNKS : (i + 1) * CHUNKS] for i in range(4))
    fetch_sem, in_sem, own_sem, send_sem, recv_sem, up_send, up_recv, down_send, down_recv = rest[4 * CHUNKS :]
    group = lax.axis_size("tile")
    groups = lax.axis_size("acq")
    tile = lax.axis_index("tile")
    acq = lax.axis_index("acq")
    parts, az_rows, rg_cols = slc_ref.shape[1:]
    cols = rg_cols // group
    spans = chunk_spans(cols)
    looks = cols // LR
    slots = group + 2 * MAXGAP
    pair_count = partners_ref.shape[0]
    has_down, has_up = acq > 0, acq < groups - 1

    fetch = pltpu.make_async_copy(offsets_ref, offsets, fetch_sem)
    fetch.start()
    load = pltpu.make_async_copy(slc_ref.at[0], padded.at[:, :, pl.ds(LANES, rg_cols)], in_sem)
    load.start()

    barrier = pltpu.get_barrier_semaphore()

    def greet(step, carry):
        other = flipped(tile, group - 1 - step, group)
        pl.semaphore_signal(barrier, inc=1, device_id=(acq, other), device_id_type=DEVICE)
        return carry

    lax.fori_loop(0, group - 1, greet, 0)

    @pl.when(has_down)
    def _():
        pl.semaphore_signal(barrier, inc=1, device_id=(acq - 1, tile), device_id_type=DEVICE)

    @pl.when(has_up)
    def _():
        pl.semaphore_signal(barrier, inc=1, device_id=(acq + 1, tile), device_id_type=DEVICE)

    fetch.wait()
    own = jnp.broadcast_to(
        offsets[pl.ds(acq * group + tile, 1), :].astype(jnp.float32), (az_rows, az_rows)
    )
    diagonal = lax.broadcasted_iota(jnp.int32, (az_rows, az_rows), 0) == lax.broadcasted_iota(
        jnp.int32, (az_rows, az_rows), 1
    )
    own = jnp.sum(jnp.where(diagonal, own, 0.0), axis=1, keepdims=True)
    shift = lax.broadcasted_iota(jnp.int32, (az_rows, LANES), 1) - (TAPS - 1)
    spot = shift.astype(jnp.float32) - own * (1.0 / PHASES)
    angle = jnp.pi * spot
    sinc = jnp.where(spot == 0.0, 1.0, jnp.sin(angle) / jnp.where(spot == 0.0, 1.0, angle))
    raw = sinc * (0.5 * (1.0 + jnp.cos(angle * (2.0 / TAPS))))
    raw = jnp.where(jnp.abs(spot) < TAPS // 2, raw, 0.0)
    found = raw / jnp.sum(raw, axis=1, keepdims=True)
    for d in range(2 * TAPS - 1):
        weights[d] = jnp.broadcast_to(found[:, d : d + 1], (az_rows, LANES))
    edge = jnp.zeros((parts, az_rows, LANES), padded.dtype)
    padded[:, :, pl.ds(0, LANES)] = edge
    padded[:, :, pl.ds(LANES + rg_cols, LANES)] = edge

    load.wait()

    greeted = jnp.where(has_down, 1, 0) + jnp.where(has_up, 1, 0)
    pl.semaphore_wait(barrier, group - 1 + greeted)

    def to_tile(step, chunk, other):
        return pltpu.make_async_remote_copy(
            src_ref=outgoing[chunk].at[step],
            dst_ref=extended[chunk].at[MAXGAP + tile],
            send_sem=send_sem.at[chunk, step],
            recv_sem=recv_sem.at[chunk, tile],
            device_id=(acq, other),
            device_id_type=DEVICE,
        )

    def from_tile(step, chunk, other):
        return pltpu.make_async_remote_copy(
            src_ref=outgoing[chunk].at[step],
            dst_ref=extended[chunk].at[MAXGAP + other],
            send_sem=send_sem.at[chunk, step],
            recv_sem=recv_sem.at[chunk, other],
            device_id=(acq, other),
            device_id_type=DEVICE,
        )

    def keep(chunk):
        return pltpu.make_async_copy(
            outgoing[chunk].at[group - 1], extended[chunk].at[MAXGAP + tile], own_sem.at[chunk]
        )

    def resample(step, carry):
        other = flipped(tile, group - 1 - step, group)
        begin = pl.multiple_of(other * cols, LANES)

        def row_block(index, inner):
            part = index // (az_rows // 16)
            row = pl.multiple_of(index % (az_rows // 16) * 16, 16)
            span = cols + 2 * LANES
            window = padded[part, pl.ds(row, 16), pl.ds(begin, span)].astype(jnp.float32)

            def weight(half, d):
                return jnp.concatenate([weights[d, pl.ds(row + half, 8), :]] * (span // LANES), axis=1)

            total = jnp.concatenate(
                [
                    weighted_shifts(window[:8], functools.partial(weight, 0)),
                    weighted_shifts(window[8:], functools.partial(weight, 8)),
                ],
                axis=0,
            )[:, LANES : LANES + cols].astype(jnp.bfloat16)
            for chunk, (first, width) in enumerate(spans):
                outgoing[chunk][step, part, pl.ds(row, 16), :] = total[:, first : first + width]
            return inner

        lax.fori_loop(0, parts * (az_rows // 16), row_block, 0)

        @pl.when(step < group - 1)
        def _():
            to_tile(step, 0, other).start()

        return carry

    def send(chunk, begin, end):
        def one(step, carry):
            to_tile(group - 2 - step, chunk, flipped(tile, 1 + step, group)).start()
            return carry

        lax.fori_loop(begin, end, one, 0)

    lax.fori_loop(0, group // 2, resample, 0)
    for chunk in range(1, EARLY):
        send(chunk, 0, group // 2)
    lax.fori_loop(group // 2, group, resample, 0)
    for chunk in range(1, CHUNKS):
        send(chunk, group // 2 if chunk < EARLY else 0, group - 1)
    for chunk in range(CHUNKS):
        keep(chunk).start()

    for chunk, (first, width) in enumerate(spans):
        spot = (lax.broadcasted_iota(jnp.int32, (width, 2 * looks), 0) + first) // LR
        lane = lax.broadcasted_iota(jnp.int32, (width, 2 * looks), 1)
        left = jnp.where(lane == spot, 1.0, 0.0)
        right = jnp.where(lane == spot + looks, 1.0, 0.0)
        for quarter, block in enumerate((left, left, right, -right)):
            pool[chunk][quarter * width : (quarter + 1) * width] = block.astype(jnp.bfloat16)
        for half in range(2):
            pool_power[chunk][half * width : (half + 1) * width] = (left + right).astype(jnp.bfloat16)

    def up(chunk, source):
        return pltpu.make_async_remote_copy(
            src_ref=extended[chunk].at[MAXGAP + source],
            dst_ref=extended[chunk].at[source - (group - MAXGAP)],
            send_sem=up_send.at[chunk, source - (group - MAXGAP)],
            recv_sem=up_recv.at[chunk, source - (group - MAXGAP)],
            device_id=(acq + 1, tile),
            device_id_type=DEVICE,
        )

    def down(chunk, source):
        return pltpu.make_async_remote_copy(
            src_ref=extended[chunk].at[MAXGAP + source],
            dst_ref=extended[chunk].at[MAXGAP + group + source],
            send_sem=down_send.at[chunk, source],
            recv_sem=down_recv.at[chunk, source],
            device_id=(acq - 1, tile),
            device_id_type=DEVICE,
        )

    def hand_on(chunk, source):
        @pl.when(has_up & (source >= group - MAXGAP))
        def _():
            up(chunk, source).start()

        @pl.when(has_down & (source < MAXGAP))
        def _():
            down(chunk, source).start()

    def relay(chunk):
        keep(chunk).wait()
        hand_on(chunk, tile)

        def one(index, carry):
            step = group - 2 - index
            source = flipped(tile, group - 1 - step, group)
            from_tile(step, chunk, source).wait_recv()
            hand_on(chunk, source)
            return carry

        lax.fori_loop(0, group - 1, one, 0)

    def gathered(chunk):
        @pl.when(has_down)
        def _():
            def one(index, carry):
                up(chunk, index + group - MAXGAP).wait_recv()
                return carry

            lax.fori_loop(0, MAXGAP, one, 0)

        @pl.when(has_up)
        def _():
            def one(index, carry):
                down(chunk, index).wait_recv()
                return carry

            lax.fori_loop(0, MAXGAP, one, 0)

    def slot_of(owner, k):
        return jnp.clip(partners_ref[k, acq * group + owner] - acq * group + MAXGAP, 0, slots - 1)

    def pairs(chunk):
        images = extended[chunk]

        def powers(index, carry):
            squares = []
            for k in range(slots // 2):
                image = images[index * (slots // 2) + k]
                squares.append(jnp.concatenate([image[0] * image[0], image[1] * image[1]], axis=1))
            pooled = jnp.dot(
                jnp.concatenate(squares, axis=0), pool_power[chunk][...], preferred_element_type=jnp.float32
            ).reshape(slots // 2, az_rows, 2 * looks)
            span = pl.ds(index * (slots // 2), slots // 2)
            power_sum[span] = pooled if chunk == 0 else power_sum[span] + pooled
            return carry

        lax.fori_loop(0, 2, powers, 0)

        def crosses(index, carry):
            blocks = []
            for owner in (index * OWNERS + j for j in range(OWNERS)):
                first = images[MAXGAP + owner]
                for k in range(pair_count):
                    second = images[slot_of(owner, k)]
                    blocks.append(
                        jnp.concatenate(
                            [first[0] * second[0], first[1] * second[1], first[1] * second[0], first[0] * second[1]],
                            axis=1,
                        )
                    )
            pooled = jnp.dot(
                jnp.concatenate(blocks, axis=0), pool[chunk][...], preferred_element_type=jnp.float32
            ).reshape(OWNERS, pair_count, az_rows, 2 * looks)
            span = pl.ds(index * OWNERS, OWNERS)
            cross_sum[span] = pooled if chunk == 0 else cross_sum[span] + pooled
            return carry

        lax.fori_loop(0, group // OWNERS, crosses, 0)

    relay(0)
    for chunk in range(CHUNKS):
        if chunk + 1 < CHUNKS:
            relay(chunk + 1)
        gathered(chunk)
        pairs(chunk)

    windows = az_rows // LA

    def mean(view, *lead):
        total = None
        for line in range(LA):
            value = view[(*lead, pl.ds(line, windows, stride=LA), slice(None))]
            total = value if total is None else total + value
        return total * (1.0 / (LA * LR))

    def finish(owner):
        mean_a = mean(power_sum, MAXGAP + owner)
        for k in range(partners_ref.shape[0]):
            mean_b = mean(power_sum, slot_of(owner, k))
            cross = mean(cross_sum, owner, k)
            square = cross * cross
            magnitude = jnp.sqrt(square + pltpu.roll(square, looks, 1))
            coherent = magnitude / jnp.sqrt((mean_a + 1e-06) * (mean_b + 1e-06))
            looked_ref[0, owner, k] = cross[:, :looks]
            looked_ref[1, owner, k] = pltpu.roll(cross, looks, 1)[:, :looks]
            coherent_ref[owner, k] = coherent[:, :looks]

    @pl.loop(0, group // 2)
    def _(index):
        finish(index * 2)
        finish(index * 2 + 1)

    for chunk in range(CHUNKS):

        def sent(step, carry, chunk=chunk):
            to_tile(step, chunk, flipped(tile, group - 1 - step, group)).wait_send()
            return carry

        lax.fori_loop(0, group - 1, sent, 0)

        @pl.when(has_up)
        def _(chunk=chunk):
            def one(index, carry):
                up(chunk, index + group - MAXGAP).wait_send()
                return carry

            lax.fori_loop(0, MAXGAP, one, 0)

        @pl.when(has_down)
        def _(chunk=chunk):
            def one(index, carry):
                down(chunk, index).wait_send()
                return carry

            lax.fori_loop(0, MAXGAP, one, 0)


def body(group, slc, offsets, partners):
    _, parts, az_rows, rg_cols = slc.shape
    pair_count = partners.shape[1]
    cols = rg_cols // group
    looks = cols // LR
    widths = [width for _, width in chunk_spans(cols)]
    slots = group + 2 * MAXGAP
    vmem = pl.BlockSpec(memory_space=pltpu.VMEM)
    hbm = pl.BlockSpec(memory_space=pltpu.HBM)
    dma = pltpu.SemaphoreType.DMA
    return pl.pallas_call(
        kernel,
        out_shape=(
            jax.ShapeDtypeStruct((2, group, pair_count, az_rows // LA, looks), jnp.float32),
            jax.ShapeDtypeStruct((group, pair_count, az_rows // LA, looks), jnp.float32),
        ),
        in_specs=[hbm, pl.BlockSpec(memory_space=pltpu.SMEM), hbm],
        out_specs=(vmem, vmem),
        scratch_shapes=[
            pltpu.VMEM(offsets.shape, jnp.int32),
            pltpu.VMEM((parts, az_rows, rg_cols + 2 * LANES), jnp.bfloat16),
            pltpu.VMEM((2 * TAPS - 1, az_rows, LANES), jnp.float32),
            pltpu.VMEM((group, pair_count, az_rows, 2 * looks), jnp.float32),
            pltpu.VMEM((slots, az_rows, 2 * looks), jnp.float32),
        ]
        + [pltpu.VMEM((slots, parts, az_rows, width), jnp.bfloat16) for width in widths]
        + [pltpu.VMEM((group, parts, az_rows, width), jnp.bfloat16) for width in widths]
        + [pltpu.VMEM((4 * width, 2 * looks), jnp.bfloat16) for width in widths]
        + [pltpu.VMEM((2 * width, 2 * looks), jnp.bfloat16) for width in widths]
        + [
            dma(()),
            dma(()),
            dma((CHUNKS,)),
            dma((CHUNKS, group)),
            dma((CHUNKS, group)),
            dma((CHUNKS, MAXGAP)),
            dma((CHUNKS, MAXGAP)),
            dma((CHUNKS, MAXGAP)),
            dma((CHUNKS, MAXGAP)),
        ],
        compiler_params=pltpu.CompilerParams(
            collective_id=0, has_side_effects=True, vmem_limit_bytes=60 * 1024 * 1024
        ),
    )(offsets, partners.T, slc)


def solution(mesh):
    return jax.shard_map(
        functools.partial(body, mesh.shape["tile"]),
        mesh=mesh,
        in_specs=(P(("acq", "tile"), None, None, None), P(), P()),
        out_specs=(P(None, "acq", None, None, "tile"), P("acq", None, None, "tile")),
        check_vma=False,
    )
```
